256 devices in a mesh: rows: 32 (over x, z_hi, core), dp: 8 (over z_lo, y).
Axes of the slice: x: 4, y: 4, z: 8 (z_hi: 4, z_lo: 2; z = z_hi * 2 + z_lo), core: 2. Of those that a mesh axis runs over, the one named last changes fastest.
Arguments:
- inputs: bfloat16 [8, 128, 128, 768], P('dp', 'rows')
- cotangent: bfloat16 [8, 128, 128, 768], P('dp', 'rows'), may hold values from -6 to 6
- extents: int32 [8, 2], P('dp'), may hold values from 4 to 128, as said below
- weights: bfloat16 [768, 3072], P('dp')
Outputs:
- outputs: bfloat16 [8, 128, 128, 768], P('dp', 'rows')
- input_grads: bfloat16 [8, 128, 128, 768], P('dp', 'rows')
- weight_grads: float32 [768, 3072], P('dp')
The draws below stay inside these ranges and needn't reach their ends.
Inputs may be any that keep to these rules, and one draw needn't show every extreme that they name: `extents`: column 0 is a valid height of at least 4, column 1 a valid width of at least 16; some image is valid in full.
All inputs are finite; a program needn't handle non-finite values.
Results may differ from the reference program's by a relative error of at most 0.034.
Values may be sent and summed in bfloat16 or wider, within the bound.
A program may use at most 128 MiB of HBM per device.

```python
import jax
import jax.numpy as jnp
from jax import lax

D = 768
HEADS = 24
HEAD_DIM = 32
GRID_COLS = 8
ROWS_DEV = 4
WIDTH = 128
HEIGHT = 128
IMAGES = 8
N_ROWS = 32


def draw_inputs(key, part):
    key = jax.random.fold_in(key, 11)
    first_key = jax.random.fold_in(key, 0)
    shape = (IMAGES, HEIGHT, WIDTH, D)
    values = jax.random.normal(first_key, shape, jnp.float32)
    return values.astype(jnp.bfloat16)


def draw_weights(key, part):
    key = jax.random.fold_in(key, 12)
    values = jax.random.normal(key, (D, 4 * D), jnp.float32) * D ** (-0.5)
    return values.astype(jnp.bfloat16)


def draw_extents(key, part):
    key = jax.random.fold_in(key, 13)
    height_key, width_key, full_key = jax.random.split(key, 3)
    heights = jax.random.randint(height_key, (IMAGES,), ROWS_DEV, HEIGHT + 1)
    widths = jax.random.randint(width_key, (IMAGES,), WIDTH // GRID_COLS, WIDTH + 1)
    chosen = jax.random.randint(full_key, (), 0, IMAGES)
    positions = jnp.arange(IMAGES, dtype=jnp.int32)
    heights = jnp.where(positions == chosen, HEIGHT, heights)
    widths = jnp.where(positions == chosen, WIDTH, widths)
    return jnp.stack([heights, widths], axis=1).astype(jnp.int32)


def block_scale(key, shape, pieces, low, high):
    def one(position, shards_of):
        steps = jax.random.uniform(jax.random.fold_in(jax.random.fold_in(key, 6), position), (shards_of,), jnp.float32, low / len(pieces), high / len(pieces))
        return jnp.repeat(jnp.exp(steps), shape[position] // shards_of).reshape((-1,) + (1,) * (len(shape) - position - 1))

    gain = one(*pieces[0])
    for cut in pieces[1:]:
        gain = gain * one(*cut)
    return gain


def scatter_about(rng, dims, deviation, reach, shards=(), kind=jnp.bfloat16):
    drawn = jax.random.normal(rng, dims, jnp.float32) * deviation
    if len(shards) > 0:
        drawn = block_scale(rng, dims, shards, -0.22, 0.18) * drawn
    return jnp.clip(drawn, min=-reach, max=reach).astype(kind)


def setup_inputs(seed: int = 0) -> dict:
    key_of = jax.random.split(jax.random.key(seed), 5)
    return {
        "inputs": draw_inputs(jax.random.fold_in(key_of[4], 71), 0),
        "cotangent": scatter_about(key_of[1], (IMAGES, HEIGHT, WIDTH, D), 1.0, 6.0, ((0, 8), (1, 32))),
        "extents": draw_extents(jax.random.fold_in(key_of[4], 71), 0),
        "weights": draw_weights(jax.random.fold_in(key_of[4], 71), 0),
    }


epsilon = 1e-05

def to_low(value):
    return lax.optimization_barrier(value.astype(jnp.bfloat16))

def normalize(tokens):
    widened = tokens.astype(jnp.float32)
    centered = widened - lax.optimization_barrier(jnp.mean(widened, axis=-1, keepdims=True))
    inv_std = lax.rsqrt(lax.optimization_barrier(jnp.mean(centered * centered, axis=-1, keepdims=True)) + epsilon)
    return (centered * inv_std, inv_std)

def to_groups(values):
    channels = values.shape[-1]
    col_groups = WIDTH // GRID_COLS
    shaped = values.reshape(N_ROWS, ROWS_DEV, GRID_COLS, col_groups, channels)
    shaped = shaped.transpose(1, 3, 0, 2, 4)
    return shaped.reshape(ROWS_DEV * col_groups, N_ROWS * GRID_COLS, channels)

def from_groups(values):
    channels = values.shape[-1]
    col_groups = WIDTH // GRID_COLS
    shaped = values.reshape(ROWS_DEV, col_groups, N_ROWS, GRID_COLS, channels)
    return shaped.transpose(2, 0, 3, 1, 4).reshape(HEIGHT * WIDTH, channels)

def group_attention(queries, key_vecs, value_vecs, key_valid, out_grad):
    members = queries.shape[0]
    inv_root = HEAD_DIM ** (-0.5)
    query_heads = queries.astype(jnp.float32).reshape(members, HEADS, HEAD_DIM)
    key_heads = key_vecs.astype(jnp.float32).reshape(members, HEADS, HEAD_DIM)
    value_heads = value_vecs.astype(jnp.float32).reshape(members, HEADS, HEAD_DIM)
    grad_heads = out_grad.astype(jnp.float32).reshape(members, HEADS, HEAD_DIM)
    scores = jnp.einsum('mhe,nhe->hmn', query_heads, key_heads) * inv_root
    scores = jnp.where(key_valid[None, None, :], scores, -jnp.inf)
    top_score = lax.optimization_barrier(jnp.max(scores, axis=-1, keepdims=True))
    shifted = jnp.exp(scores - top_score)
    chances = shifted / lax.optimization_barrier(jnp.sum(shifted, axis=-1, keepdims=True))
    chances_low = to_low(chances).astype(jnp.float32)
    attended = to_low(jnp.einsum('hmn,nhe->mhe', chances_low, value_heads))
    chance_grad = jnp.einsum('mhe,nhe->hmn', grad_heads, value_heads)
    value_grad = to_low(jnp.einsum('hmn,mhe->nhe', chances_low, grad_heads))
    spread = lax.optimization_barrier(jnp.sum(chances * chance_grad, axis=-1, keepdims=True))
    score_grad = to_low(chances * (chance_grad - spread) * inv_root).astype(jnp.float32)
    query_grad = to_low(jnp.einsum('hmn,nhe->mhe', score_grad, key_heads))
    key_grad = to_low(jnp.einsum('hmn,mhe->nhe', score_grad, query_heads))
    return (attended.reshape(members, D), query_grad.reshape(members, D), key_grad.reshape(members, D), value_grad.reshape(members, D))

def one_image(image, grad_image, extent, weights):
    token_count = HEIGHT * WIDTH
    row_ids = lax.broadcasted_iota(jnp.int32, (HEIGHT, WIDTH, 1), 0)
    col_ids = lax.broadcasted_iota(jnp.int32, (HEIGHT, WIDTH, 1), 1)
    valid = jnp.logical_and(row_ids < extent[0], col_ids < extent[1])
    flat_in = image.reshape(token_count, D)
    unit_rows, inv_std = normalize(flat_in)
    normed = to_low(unit_rows)
    in_weights = weights[:, :3 * D]
    out_weights = weights[:, 3 * D:]
    projected = to_low(jnp.dot(normed, in_weights, preferred_element_type=jnp.float32))
    masked_grad = grad_image.reshape(token_count, D) * valid.reshape(token_count, 1).astype(jnp.bfloat16)
    out_grad = to_low(jnp.dot(masked_grad, out_weights.T, preferred_element_type=jnp.float32))
    stacked = to_groups(jnp.concatenate([projected, out_grad], axis=1).reshape(HEIGHT, WIDTH, 4 * D))
    key_valid = to_groups(valid)[:, :, 0]

    def per_group(group_item):
        block, mask_row = group_item
        return group_attention(block[:, :D], block[:, D:2 * D], block[:, 2 * D:3 * D], mask_row, block[:, 3 * D:])
    attended, query_grad, key_grad, value_grad = lax.map(per_group, (stacked, key_valid))
    attended = from_groups(attended)
    proj_grad = jnp.concatenate([from_groups(query_grad), from_groups(key_grad), from_groups(value_grad)], axis=1)
    outputs = to_low(flat_in.astype(jnp.float32) + jnp.dot(attended, out_weights, preferred_element_type=jnp.float32))
    unit_grad = jnp.dot(proj_grad, in_weights.T, preferred_element_type=jnp.float32)
    input_grads = masked_grad.astype(jnp.float32) + inv_std * (unit_grad - lax.optimization_barrier(jnp.mean(unit_grad, axis=-1, keepdims=True)) - unit_rows * lax.optimization_barrier(jnp.mean(unit_grad * unit_rows, axis=-1, keepdims=True)))
    weight_term = jnp.concatenate([jnp.dot(normed.T, proj_grad, preferred_element_type=jnp.float32), jnp.dot(attended.T, masked_grad, preferred_element_type=jnp.float32)], axis=1)
    return (outputs.reshape(HEIGHT, WIDTH, D), to_low(input_grads).reshape(HEIGHT, WIDTH, D), weight_term)

def reference(inputs, cotangent, extents, weights):

    def step_image(carried, image_item):
        image, grad_image, extent = image_item
        outputs, input_grads, weight_term = one_image(image, grad_image, extent, weights)
        return (carried + weight_term, (outputs, input_grads))
    start_sum = jnp.zeros((D, 4 * D), jnp.float32)
    total, (outputs, input_grads) = lax.scan(step_image, start_sum, (inputs, cotangent, extents))
    return (outputs, input_grads, total)
```

```python
import math

import jax
import jax.numpy as jnp
from jax import lax
from jax.experimental import pallas as pl
from jax.experimental.pallas import tpu as pltpu
from jax.sharding import PartitionSpec as P

MESH = pl.DeviceIdType.MESH
BF16 = jnp.bfloat16
F32 = jnp.float32

D = 768
HEADS = 24
HEAD_DIM = 32
TOKENS = 512
MEMBERS = 256
HALF = 384
ROOT = HEAD_DIM ** (-0.5)
EPSILON = 1e-05

CONTRACT_LAST = (((1,), (1,)), ((), ()))


def dot(a, b):
    return jnp.dot(a, b, preferred_element_type=F32)


def dot_last(a, b):
    return lax.dot_general(a, b, CONTRACT_LAST, preferred_element_type=F32)


def split(block):
    wide = block.astype(F32).reshape(8, 16, block.shape[-1])
    return [wide[:, 8 * g : 8 * g + 8, :].reshape(64, block.shape[-1]) for g in range(2)]


def merge(first, second):
    parts = [p.reshape(8, 8, p.shape[-1]) for p in (first, second)]
    return jnp.concatenate(parts, axis=1).reshape(128, first.shape[-1])


def kernel(
    extent_ref,
    x_ref,
    g_ref,
    w_ref,
    out_ref,
    ig_ref,
    wg_ref,
    sent,
    came,
    weights,
    unit,
    inv,
    normed_t,
    qkv,
    kv_t,
    bias,
    chances,
    att_t,
    att,
    masked,
    out_grad,
    proj_grad,
    wide,
    terms,
    core_in,
    core_sum,
    y_in,
    y_sum,
    x_in,
    x_sum,
    z_in,
    total,
    whole,
    a_send,
    a_recv,
    w_send,
    w_recv,
    r_send,
    r_recv,
):
    rows_at = lax.axis_index("rows")
    dp_at = lax.axis_index("dp")
    x_at, zh, core = rows_at // 8, (rows_at // 2) % 4, rows_at % 2
    zl, y_at = dp_at // 4, dp_at % 4

    def device(x=None, h=None, c=None, l=None, y=None):
        x = x_at if x is None else x
        h = zh if h is None else h
        c = core if c is None else c
        l = zl if l is None else l
        y = y_at if y is None else y
        return (x * 8 + h * 2 + c, l * 4 + y)

    def push(src, dst, send, recv, to):
        pltpu.make_async_remote_copy(
            src_ref=src, dst_ref=dst, send_sem=send, recv_sem=recv, device_id=to, device_id_type=MESH
        ).start()

    def wait(ref, sem):
        pltpu.make_async_copy(ref, ref, sem).wait()

    def at16(i, size=16):
        return pl.ds(pl.multiple_of(i * 16, 16), size)

    for b in range(3):
        for n in range(3):
            weights[b, dp_at, :, pl.ds(n * 256, 256)] = w_ref[:, pl.ds(n * D + b * 256, 256)]
    weights[3, dp_at] = w_ref[:, pl.ds(3 * D, D)]
    barrier = pltpu.get_barrier_semaphore()

    @pl.loop(1, 32)
    def _(k):
        pl.semaphore_signal(
            barrier, inc=1, device_id=((rows_at + k) % 32, dp_at), device_id_type=MESH
        )

    @pl.loop(1, 8)
    def _(k):
        pl.semaphore_signal(
            barrier, inc=1, device_id=(rows_at, (dp_at + k) % 8), device_id_type=MESH
        )

    side = (zh + 3 + 2 * zl) % 4

    @pl.loop(1, 4)
    def _(k):
        for to in (
            device(x=(x_at + 1) % 4, y=(y_at + k) % 4),
            device(x=(x_at + 2) % 4, y=(y_at + k) % 4),
            device(x=(x_at + 3) % 4, y=(y_at + k) % 4),
            device(h=(zh + k) % 4, l=1 - zl),
            device(h=side, l=1 - zl, y=(y_at + k) % 4),
        ):
            pl.semaphore_signal(barrier, inc=1, device_id=to, device_id_type=MESH)

    to_row = lax.broadcasted_iota(jnp.int32, (128, 128), 0)
    from_row = lax.broadcasted_iota(jnp.int32, (128, 128), 1)
    gather = (from_row == (to_row % 8) * 16 + to_row // 8).astype(BF16)
    scatter = (from_row == (to_row % 16) * 8 + to_row // 16).astype(BF16)

    def reorder(matrix, src, dst):
        for i in range(4):
            part = pl.ds(128 * i, 128)
            dst[part, :] = dot(matrix, src[part, :]).astype(BF16)

    def exchange(t, part=0, first=1, last=32):
        @pl.loop(first, last)
        def _(k):
            kc, kx, kz = k // 16, (k // 4) % 4, k % 4
            peer = ((x_at + kx) % 4) * 8 + ((zh + kz) % 4) * 2 + (core + kc) % 2
            push(
                sent.at[t, at16(peer)],
                came.at[t, at16(rows_at)],
                a_send.at[t, part],
                a_recv.at[t],
                (peer, dp_at),
            )

        if part == 0:
            came[t, at16(rows_at), :] = sent[t, at16(rows_at), :]

    def left(t, part, count):
        wait(came.at[t, pl.ds(0, 16 * count)], a_send.at[t, part])

    def arrive(t):
        wait(came.at[t, pl.ds(0, 496)], a_recv.at[t])

    reorder(gather, x_ref, sent.at[0])
    pl.semaphore_wait(barrier, 53)

    piece = (pl.ds(pl.multiple_of((x_at // 2) * 48, 16), 48), pl.ds(pl.multiple_of((x_at % 2) * HALF, 128), HALF))
    near, far = pl.ds(zl * 4, 4), pl.ds((1 - zl) * 4, 4)

    def weights_far(p):
        mine = weights.at[2 * p + core, dp_at, piece[0], piece[1]]
        for k in range(4):
            to = device(h=zh if k < 2 else side, l=1 - zl, y=(y_at + k) % 4)
            push(mine, mine, w_send.at[p, 0], w_recv.at[p, 0], to)

    def weights_near(p):
        mine = weights.at[2 * p + core, dp_at]
        for k in range(1, 4):
            push(mine, mine, w_send.at[p, 1], w_recv.at[p, 1], device(y=(y_at + k) % 4))

    def weights_across(p):
        mine = weights.at[2 * p + core, far, piece[0], piece[1]]
        wait(mine, w_recv.at[p, 0])
        for k in range(1, 4):
            push(mine, mine, w_send.at[p, 2], w_recv.at[p, 2], device(x=(x_at + k) % 4))

    def weights_core_near(p):
        mine = weights.at[2 * p + core, near]
        wait(weights.at[2 * p, pl.ds(0, 3)], w_recv.at[p, 1])
        push(mine, mine, w_send.at[p, 3], w_recv.at[p, 3], device(c=1 - core))

    def weights_core_far(p):
        mine = weights.at[2 * p + core, far]
        wait(weights.at[2 * p, pl.ds(0, 3)], w_recv.at[p, 2])
        push(mine, mine, w_send.at[p, 4], w_recv.at[p, 4], device(c=1 - core))

    def weights_there(p):
        wait(weights.at[2 * p, near], w_recv.at[p, 3])
        wait(weights.at[2 * p, far], w_recv.at[p, 4])

    def weights_settle(p):
        wait(weights.at[2 * p, far, piece[0], piece[1]], w_send.at[p, 0])
        wait(weights.at[2 * p, pl.ds(0, 3)], w_send.at[p, 1])
        wait(weights.at[2 * p, pl.ds(0, 3)], w_send.at[p, 2])
        wait(weights.at[2 * p, near], w_send.at[p, 3])
        wait(weights.at[2 * p, far], w_send.at[p, 4])

    def block_weights(b):
        return weights[b].reshape(D, D)

    weights_far(0)
    weights_near(0)
    exchange(0)
    weights_across(0)
    weights_far(1)
    weights_near(1)
    reorder(gather, g_ref, sent.at[1])
    weights_core_near(0)
    weights_across(1)
    weights_core_far(0)
    weights_core_near(1)

    height, width = extent_ref[0, 0], extent_ref[0, 1]
    member = lax.broadcasted_iota(jnp.int32, (MEMBERS, 128), 0)
    row_ids = 4 * (member // 8) + rows_at // 8
    for g in range(2):
        col_ids = 16 * (member % 8) + 2 * (rows_at % 8) + g
        valid = jnp.logical_and(row_ids < height, col_ids < width)
        bias[g] = jnp.where(valid, 0.0, -jnp.inf).astype(F32)

    arrive(0)
    exchange(1)

    @pl.loop(0, 4)
    def _(i):
        tokens = split(came[0, pl.ds(pl.multiple_of(i * 128, 128), 128), :])
        for g in range(2):
            part = pl.ds(pl.multiple_of(g * MEMBERS + i * 64, 64), 64)
            centered = tokens[g] - jnp.mean(tokens[g], axis=-1, keepdims=True)
            scale = lax.rsqrt(jnp.mean(centered * centered, axis=-1, keepdims=True) + EPSILON)
            unit_rows = centered * scale
            unit[part, :] = unit_rows
            inv[part, :] = jnp.broadcast_to(scale, (64, 128))
            att[part, :] = unit_rows.astype(BF16)

    @pl.loop(0, 6)
    def _(i):
        part = pl.ds(pl.multiple_of(i * 128, 128), 128)
        normed_t[part, :] = att[:, part].T

    lane = lax.broadcasted_iota(jnp.int32, (MEMBERS, 128), 1) // HEAD_DIM
    to_exp2 = ROOT * math.log2(math.e)

    def one_head(value, j):
        return jnp.where(lane == j, value, jnp.zeros_like(value))

    def feature(i, size=128):
        return pl.ds(pl.multiple_of(i, size), size)

    def project(block):
        for n in range(3):
            tile = dot(att[...], weights[block, :, :, pl.ds(256 * n, 256)].reshape(D, 256)).astype(BF16)
            qkv[:, pl.ds(block * D + 256 * n, 256)] = tile
            if n > 0:
                kv_t[block, pl.ds(256 * (n - 1), 256), :] = tile.T

    def attend(block):
        @pl.loop(0, 4)
        def _(i):
            g, quad = i // 2, i % 2
            mine = feature(g * MEMBERS, MEMBERS)
            queries = qkv[mine, feature(block * D + quad * 128)]
            keys = qkv[mine, feature(block * D + 256 + quad * 128)]
            shift = bias[g]
            shift = jnp.concatenate([shift, shift], axis=1)
            for j in range(4):
                scores = dot_last(one_head(keys, j), queries) * to_exp2 + shift
                shifted = jnp.exp2(scores - jnp.max(scores, axis=0, keepdims=True))
                low = (shifted * (1.0 / jnp.sum(shifted, axis=0, keepdims=True))).astype(BF16)
                chances[(block * 4 + i) * 4 + j] = low
                values_t = kv_t[block, feature(256 + quad * 128 + j * 32, 32), mine]
                att_t[feature(block * 256 + quad * 128 + j * 32, 32), mine] = dot(values_t, low).astype(BF16)

    weights_there(0)
    project(0)
    project(1)
    attend(0)
    weights_core_far(1)
    attend(1)
    weights_there(1)
    project(2)
    attend(2)

    @pl.loop(0, 6)
    def _(i):
        part = feature(i * 128)
        att[:, part] = att_t[part, :].T

    for i in range(3):
        part = pl.ds(256 * i, 256)
        wide[:, part] = dot(att[...], weights[3, :, :, part].reshape(D, 256))

    @pl.loop(0, 4)
    def _(i):
        both = feature(i * 128)
        first = wide[feature(i * 64, 64), :]
        second = wide[feature(MEMBERS + i * 64, 64), :]
        sent[2, both, :] = (came[0, both, :].astype(F32) + merge(first, second)).astype(BF16)

    exchange(2)

    active = zl == x_at // 2
    owner = jnp.logical_and(active, zh < 3)
    mine48 = pl.ds(pl.multiple_of((x_at % 2) * 48, 16), 48)

    def start_core(b):
        push(
            terms.at[b, :, pl.ds(pl.multiple_of((1 - core) * HALF, 128), HALF)],
            core_in.at[b],
            r_send.at[b, 0],
            r_recv.at[b, 0],
            device(c=1 - core),
        )

    def start_y(b):
        wait(core_in.at[b], r_recv.at[b, 0])
        for l in range(2):
            for y in range(4):
                src, dst = pl.ds((l * 4 + y) * 96, 96), pl.ds((y * 2 + l) * 96, 96)
                cols = pl.ds(pl.multiple_of(core * HALF, 128), HALF)
                core_sum[b, dst, :] = (
                    terms[b, src, cols].astype(F32) + core_in[b, src, :].astype(F32)
                ).astype(BF16)

        for k in range(1, 4):
            y = (y_at + k) % 4
            src = core_sum.at[b, pl.ds(pl.multiple_of(y * 192, 16), 192)]
            push(src, y_in.at[b, k - 1], r_send.at[b, 1], r_recv.at[b, 1], device(y=y))

    def start_x(b):
        wait(y_in.at[b], r_recv.at[b, 1])
        acc = core_sum[b, pl.ds(pl.multiple_of(y_at * 192, 16), 192), :].astype(F32)
        for k in range(3):
            acc = acc + y_in[b, k].astype(F32)
        y_sum[b] = acc.astype(BF16)
        for k in range(1, 4):
            x = (x_at + k) % 4
            src = y_sum.at[b, pl.ds(pl.multiple_of(x * 48, 16), 48)]
            push(src, x_in.at[b, k - 1], r_send.at[b, 5], r_recv.at[b, 5], device(x=x))

    def start_z(b):
        wait(x_in.at[b], r_recv.at[b, 5])
        acc = y_sum[b, pl.ds(pl.multiple_of(x_at * 48, 16), 48), :].astype(F32)
        for k in range(3):
            acc = acc + x_in[b, k].astype(F32)
        x_sum[b] = acc.astype(BF16)
        for j in range(3):
            rows = pl.ds(16 * j, 16)

            @pl.when(jnp.logical_not(jnp.logical_and(active, zh == j)))
            def _():
                to = device(h=j, l=x_at // 2)
                push(x_sum.at[b, rows], z_in.at[b, zh * 2 + zl], r_send.at[b, 2], r_recv.at[b, 2], to)

            @pl.when(jnp.logical_and(active, zh == j))
            def _():
                z_in[b, zh * 2 + zl] = x_sum[b, rows, :]

    def start_regather(b):
        @pl.when(owner)
        def _():
            wait(z_in.at[b, pl.ds(0, 7)], r_recv.at[b, 2])
            acc = z_in[b, 0].astype(F32)
            for k in range(1, 8):
                acc = acc + z_in[b, k].astype(F32)
            rows = pl.ds(pl.multiple_of(zh * 16, 16), 16)
            total[b, rows, :] = acc.astype(BF16)
            for k in range(1, 4):
                to = device(h=(zh + k) % 4)
                push(total.at[b, rows], total.at[b, rows], r_send.at[b, 3], r_recv.at[b, 3], to)

    def start_spread(b):
        @pl.when(active)
        def _():
            @pl.when(zh < 3)
            def _():
                wait(total.at[b, pl.ds(0, 32)], r_recv.at[b, 3])

            @pl.when(zh == 3)
            def _():
                wait(total.at[b], r_recv.at[b, 3])

            for k in range(1, 8):
                to = device(x=(x_at + k // 2) % 4, c=(core + k) % 2)
                push(total.at[b], whole.at[b, core, mine48], r_send.at[b, 4], r_recv.at[b, 4], to)
            whole[b, core, mine48, :] = total[b]

    def finish_terms(b):
        @pl.when(active)
        def _():
            wait(core_in.at[b, pl.ds(0, 144)], r_recv.at[b, 4])

        @pl.when(jnp.logical_not(active))
        def _():
            wait(core_in.at[b, pl.ds(0, 192)], r_recv.at[b, 4])

        full = jnp.concatenate([whole[b, 0].astype(F32), whole[b, 1].astype(F32)], axis=1)
        if b == 0:
            wg_ref[:, pl.ds(3 * D, D)] = full
        else:
            for n in range(3):
                wg_ref[:, pl.ds(n * D + (b - 1) * 256, 256)] = full[:, n * 256 : (n + 1) * 256]

    def settle_terms(b):
        wait(core_in.at[b], r_send.at[b, 0])
        wait(y_in.at[b], r_send.at[b, 1])
        wait(x_in.at[b], r_send.at[b, 5])

        @pl.when(owner)
        def _():
            wait(z_in.at[b, pl.ds(0, 2)], r_send.at[b, 2])
            wait(z_in.at[b, pl.ds(0, 3)], r_send.at[b, 3])

        @pl.when(jnp.logical_not(owner))
        def _():
            wait(z_in.at[b, pl.ds(0, 3)], r_send.at[b, 2])

        @pl.when(active)
        def _():
            wait(core_in.at[b, pl.ds(0, 336)], r_send.at[b, 4])

    arrive(1)

    @pl.loop(0, 4)
    def _(i):
        grads = split(came[1, feature(i * 128), :])
        for g in range(2):
            part = feature(g * MEMBERS + i * 64, 64)
            keep = bias[g, feature(i * 64, 64), :] == 0.0
            keep = jnp.concatenate([keep.astype(F32)] * 6, axis=1)
            masked[part, :] = (grads[g] * keep).astype(BF16)

    for i in range(3):
        part = pl.ds(256 * i, 256)
        out_grad[:, part] = dot_last(masked[...], block_weights(3)[256 * i : 256 * i + 256]).astype(BF16)
    for i in range(3):
        part = pl.ds(256 * i, 256)
        terms[0, :, part] = dot(att_t[...], masked[:, part]).astype(BF16)
    start_core(0)

    def attend_back(block, g):
        @pl.loop(0, 2)
        def _(quad):
            mine = feature(g * MEMBERS, MEMBERS)
            queries = qkv[mine, feature(block * D + quad * 128)]
            values = qkv[mine, feature(block * D + 512 + quad * 128)]
            grads = out_grad[mine, feature(block * 256 + quad * 128)]
            key_grad = jnp.zeros((MEMBERS, 128), F32)
            value_grad = jnp.zeros((MEMBERS, 128), F32)
            query_grad = []
            for j in range(4):
                chance_grad = dot_last(one_head(values, j), grads)
                low = chances[(block * 4 + g * 2 + quad) * 4 + j]
                chance = low.astype(F32)
                spread = jnp.sum(chance * chance_grad, axis=0, keepdims=True)
                score_grad = (chance * (chance_grad - spread) * ROOT).astype(BF16)
                value_grad += dot(low, one_head(grads, j))
                key_grad += dot(score_grad, one_head(queries, j))
                keys_t = kv_t[block, feature(quad * 128 + j * 32, 32), mine]
                query_grad.append(dot(keys_t, score_grad))
            query_grad = jnp.concatenate(query_grad, axis=0).astype(BF16)
            proj_grad[mine, feature(block * D + quad * 128)] = query_grad.T
            proj_grad[mine, feature(block * D + 256 + quad * 128)] = key_grad.astype(BF16)
            proj_grad[mine, feature(block * D + 512 + quad * 128)] = value_grad.astype(BF16)

    def weight_terms(block):
        for n in range(3):
            cols = pl.ds(block * D + n * 256, 256)
            terms[block + 1, :, pl.ds(n * 256, 256)] = dot(normed_t[...], proj_grad[:, cols]).astype(BF16)

    attend_back(0, 0)
    start_y(0)
    attend_back(0, 1)
    weight_terms(0)
    start_core(1)
    attend_back(1, 0)
    start_x(0)
    start_y(1)
    attend_back(1, 1)
    weight_terms(1)
    start_core(2)
    start_z(0)
    attend_back(2, 0)
    start_x(1)
    start_y(2)
    start_regather(0)
    attend_back(2, 1)
    weight_terms(2)
    start_core(3)
    start_z(1)
    start_spread(0)
    for i in range(3):
        part = pl.ds(256 * i, 256)
        grad = jnp.zeros((TOKENS, 256), F32)
        for b in range(3):
            grad += dot_last(proj_grad[:, pl.ds(b * D, D)], block_weights(b)[256 * i : 256 * i + 256])
        wide[:, part] = grad
    start_y(3)
    start_x(2)

    @pl.loop(0, 4)
    def _(i):
        both = feature(i * 128)
        parts = []
        for g in range(2):
            part = feature(g * MEMBERS + i * 64, 64)
            grad, unit_rows = wide[part, :], unit[part, :]
            moved = (
                grad
                - jnp.mean(grad, axis=-1, keepdims=True)
                - unit_rows * jnp.mean(grad * unit_rows, axis=-1, keepdims=True)
            )
            scale = jnp.concatenate([inv[part, :]] * 6, axis=1)
            parts.append(masked[part, :].astype(F32) + scale * moved)
        sent[3, both, :] = merge(*parts).astype(BF16)

    start_regather(1)
    start_z(2)
    exchange(3, 0, 1, 8)
    exchange(3, 1, 8, 16)
    start_x(3)
    arrive(2)
    reorder(scatter, came.at[2], out_ref)
    start_spread(1)
    finish_terms(0)
    left(3, 0, 7)
    start_regather(2)
    start_z(3)
    exchange(3, 2, 16, 24)
    finish_terms(1)
    left(3, 1, 8)
    exchange(3, 3, 24, 32)
    start_spread(2)
    start_regather(3)
    finish_terms(2)
    start_spread(3)
    finish_terms(3)
    arrive(3)
    reorder(scatter, came.at[3], ig_ref)
    left(3, 2, 8)
    left(3, 3, 8)

    for t in range(4):
        if t < 3:
            left(t, 0, 31)
        settle_terms(t)
    for p in range(2):
        weights_settle(p)


def per_device(inputs, cotangent, extents, weights):
    shape = inputs.shape
    vmem = pl.BlockSpec(memory_space=pltpu.VMEM)
    out, ig, wg = pl.pallas_call(
        kernel,
        out_shape=(
            jax.ShapeDtypeStruct((TOKENS, D), BF16),
            jax.ShapeDtypeStruct((TOKENS, D), BF16),
            jax.ShapeDtypeStruct((96, 4 * D), F32),
        ),
        in_specs=[pl.BlockSpec(memory_space=pltpu.SMEM), vmem, vmem, vmem],
        out_specs=(vmem, vmem, vmem),
        scratch_shapes=[
            pltpu.VMEM((4, TOKENS, D), BF16),
            pltpu.VMEM((4, TOKENS, D), BF16),
            pltpu.VMEM((4, 8, 96, D), BF16),
            pltpu.VMEM((TOKENS, D), F32),
            pltpu.VMEM((TOKENS, 128), F32),
            pltpu.VMEM((D, TOKENS), BF16),
            pltpu.VMEM((TOKENS, 3 * D), BF16),
            pltpu.VMEM((3, TOKENS, TOKENS), BF16),
            pltpu.VMEM((2, MEMBERS, 128), F32),
            pltpu.VMEM((2 * HEADS, MEMBERS, MEMBERS), BF16),
            pltpu.VMEM((D, TOKENS), BF16),
            pltpu.VMEM((TOKENS, D), BF16),
            pltpu.VMEM((TOKENS, D), BF16),
            pltpu.VMEM((TOKENS, D), BF16),
            pltpu.VMEM((TOKENS, 3 * D), BF16),
            pltpu.VMEM((TOKENS, D), F32),
            pltpu.VMEM((4, D, D), BF16),
            pltpu.VMEM((4, D, HALF), BF16),
            pltpu.VMEM((4, D, HALF), BF16),
            pltpu.VMEM((4, 3, 192, HALF), BF16),
            pltpu.VMEM((4, 192, HALF), BF16),
            pltpu.VMEM((4, 3, 48, HALF), BF16),
            pltpu.VMEM((4, 48, HALF), BF16),
            pltpu.VMEM((4, 8, 16, HALF), BF16),
            pltpu.VMEM((4, 48, HALF), BF16),
            pltpu.VMEM((4, 2, 96, HALF), BF16),
            pltpu.SemaphoreType.DMA((4, 4)),
            pltpu.SemaphoreType.DMA((4,)),
            pltpu.SemaphoreType.DMA((2, 5)),
            pltpu.SemaphoreType.DMA((2, 5)),
            pltpu.SemaphoreType.DMA((4, 6)),
            pltpu.SemaphoreType.DMA((4, 6)),
        ],
        compiler_params=pltpu.CompilerParams(
            collective_id=0, has_side_effects=True, vmem_limit_bytes=60 << 20
        ),
    )(extents, inputs.reshape(TOKENS, D), cotangent.reshape(TOKENS, D), weights)
    return out.reshape(shape), ig.reshape(shape), wg


def solution(mesh):
    placed = (
        P("dp", "rows", None, None),
        P("dp", "rows", None, None),
        P("dp", None),
        P("dp", None),
    )
    return jax.shard_map(
        per_device,
        mesh=mesh,
        in_specs=placed,
        out_specs=(P("dp", "rows", None, None), P("dp", "rows", None, None), P("dp", None)),
        check_vma=False,
    )
```

```python
import math

import jax
import jax.numpy as jnp
from jax import lax
from jax.experimental import pallas as pl
from jax.experimental.pallas import tpu as pltpu
from jax.sharding import PartitionSpec as P

MESH = pl.DeviceIdType.MESH
BF16 = jnp.bfloat16
F32 = jnp.float32

D = 768
HEADS = 24
HEAD_DIM = 32
TOKENS = 512
MEMBERS = 256
HALF = 384
ROOT = HEAD_DIM ** (-0.5)
EPSILON = 1e-05

CONTRACT_LAST = (((1,), (1,)), ((), ()))


def dot(a, b):
    return jnp.dot(a, b, preferred_element_type=F32)


def dot_last(a, b):
    return lax.dot_general(a, b, CONTRACT_LAST, preferred_element_type=F32)


def split(block):
    wide = block.astype(F32).reshape(8, 16, block.shape[-1])
    return [wide[:, 8 * g : 8 * g + 8, :].reshape(64, block.shape[-1]) for g in range(2)]


def merge(first, second):
    parts = [p.reshape(8, 8, p.shape[-1]) for p in (first, second)]
    return jnp.concatenate(parts, axis=1).reshape(128, first.shape[-1])


def kernel(
    extent_ref,
    x_ref,
    g_ref,
    w_ref,
    out_ref,
    ig_ref,
    wg_ref,
    sent,
    came,
    weights,
    unit,
    inv,
    normed_t,
    qkv,
    kv_t,
    bias,
    chances,
    att_t,
    att,
    masked,
    out_grad,
    proj_grad,
    wide,
    terms,
    core_in,
    core_sum,
    y_in,
    y_sum,
    x_in,
    x_sum,
    z_in,
    xy_in,
    all_in,
    total,
    whole,
    a_send,
    a_recv,
    w_send,
    w_recv,
    r_send,
    r_recv,
):
    rows_at = lax.axis_index("rows")
    dp_at = lax.axis_index("dp")
    x_at, zh, core = rows_at // 8, (rows_at // 2) % 4, rows_at % 2
    zl, y_at = dp_at // 4, dp_at % 4

    def device(x=None, h=None, c=None, l=None, y=None):
        x = x_at if x is None else x
        h = zh if h is None else h
        c = core if c is None else c
        l = zl if l is None else l
        y = y_at if y is None else y
        return (x * 8 + h * 2 + c, l * 4 + y)

    def push(src, dst, send, recv, to):
        pltpu.make_async_remote_copy(
            src_ref=src, dst_ref=dst, send_sem=send, recv_sem=recv, device_id=to, device_id_type=MESH
        ).start()

    def wait(ref, sem):
        pltpu.make_async_copy(ref, ref, sem).wait()

    def at16(i, size=16):
        return pl.ds(pl.multiple_of(i * 16, 16), size)

    for b in range(3):
        for n in range(3):
            weights[b, dp_at, :, pl.ds(n * 256, 256)] = w_ref[:, pl.ds(n * D + b * 256, 256)]
    weights[3, dp_at] = w_ref[:, pl.ds(3 * D, D)]
    barrier = pltpu.get_barrier_semaphore()

    @pl.loop(1, 32)
    def _(k):
        pl.semaphore_signal(
            barrier, inc=1, device_id=((rows_at + k) % 32, dp_at), device_id_type=MESH
        )

    @pl.loop(1, 8)
    def _(k):
        pl.semaphore_signal(
            barrier, inc=1, device_id=(rows_at, (dp_at + k) % 8), device_id_type=MESH
        )

    side = (zh + 3 + 2 * zl) % 4

    @pl.loop(1, 4)
    def _(k):
        for to in (
            device(x=(x_at + 1) % 4, y=(y_at + k) % 4),
            device(x=(x_at + 2) % 4, y=(y_at + k) % 4),
            device(x=(x_at + 3) % 4, y=(y_at + k) % 4),
            device(h=(zh + k) % 4, l=1 - zl),
            device(h=side, l=1 - zl, y=(y_at + k) % 4),
        ):
            pl.semaphore_signal(barrier, inc=1, device_id=to, device_id_type=MESH)

    to_row = lax.broadcasted_iota(jnp.int32, (128, 128), 0)
    from_row = lax.broadcasted_iota(jnp.int32, (128, 128), 1)
    gather = (from_row == (to_row % 8) * 16 + to_row // 8).astype(BF16)
    scatter = (from_row == (to_row % 16) * 8 + to_row // 16).astype(BF16)

    def reorder(matrix, src, dst):
        for i in range(4):
            part = pl.ds(128 * i, 128)
            dst[part, :] = dot(matrix, src[part, :]).astype(BF16)

    def exchange(t, part=0, first=1, last=32):
        @pl.loop(first, last)
        def _(k):
            kc, kx, kz = k // 16, (k // 4) % 4, k % 4
            peer = ((x_at + kx) % 4) * 8 + ((zh + kz) % 4) * 2 + (core + kc) % 2
            push(
                sent.at[t, at16(peer)],
                came.at[t, at16(rows_at)],
                a_send.at[t, part],
                a_recv.at[t],
                (peer, dp_at),
            )

        if part == 0:
            came[t, at16(rows_at), :] = sent[t, at16(rows_at), :]

    def left(t, part, count):
        wait(came.at[t, pl.ds(0, 16 * count)], a_send.at[t, part])

    def arrive(t):
        wait(came.at[t, pl.ds(0, 496)], a_recv.at[t])

    reorder(gather, x_ref, sent.at[0])
    pl.semaphore_wait(barrier, 53)

    piece = (pl.ds(pl.multiple_of((x_at // 2) * 48, 16), 48), pl.ds(pl.multiple_of((x_at % 2) * HALF, 128), HALF))
    near, far = pl.ds(zl * 4, 4), pl.ds((1 - zl) * 4, 4)

    def weights_far(p):
        mine = weights.at[2 * p + core, dp_at, piece[0], piece[1]]
        for k in range(4):
            to = device(h=zh if k < 2 else side, l=1 - zl, y=(y_at + k) % 4)
            push(mine, mine, w_send.at[p, 0], w_recv.at[p, 0], to)

    def weights_near(p):
        mine = weights.at[2 * p + core, dp_at]
        for k in range(1, 4):
            push(mine, mine, w_send.at[p, 1], w_recv.at[p, 1], device(y=(y_at + k) % 4))

    def weights_across(p):
        mine = weights.at[2 * p + core, far, piece[0], piece[1]]
        wait(mine, w_recv.at[p, 0])
        for k in range(1, 4):
            push(mine, mine, w_send.at[p, 2], w_recv.at[p, 2], device(x=(x_at + k) % 4))

    def weights_core_near(p):
        mine = weights.at[2 * p + core, near]
        wait(weights.at[2 * p, pl.ds(0, 3)], w_recv.at[p, 1])
        push(mine, mine, w_send.at[p, 3], w_recv.at[p, 3], device(c=1 - core))

    def weights_core_far(p):
        mine = weights.at[2 * p + core, far]
        wait(weights.at[2 * p, pl.ds(0, 3)], w_recv.at[p, 2])
        push(mine, mine, w_send.at[p, 4], w_recv.at[p, 4], device(c=1 - core))

    def weights_there(p):
        wait(weights.at[2 * p, near], w_recv.at[p, 3])
        wait(weights.at[2 * p, far], w_recv.at[p, 4])

    def weights_settle(p):
        wait(weights.at[2 * p, far, piece[0], piece[1]], w_send.at[p, 0])
        wait(weights.at[2 * p, pl.ds(0, 3)], w_send.at[p, 1])
        wait(weights.at[2 * p, pl.ds(0, 3)], w_send.at[p, 2])
        wait(weights.at[2 * p, near], w_send.at[p, 3])
        wait(weights.at[2 * p, far], w_send.at[p, 4])

    def block_weights(b):
        return weights[b].reshape(D, D)

    weights_far(0)
    weights_near(0)
    exchange(0)
    weights_across(0)
    weights_far(1)
    weights_near(1)
    reorder(gather, g_ref, sent.at[1])
    weights_core_near(0)
    weights_across(1)
    weights_core_far(0)
    weights_core_near(1)

    height, width = extent_ref[0, 0], extent_ref[0, 1]
    member = lax.broadcasted_iota(jnp.int32, (MEMBERS, 128), 0)
    row_ids = 4 * (member // 8) + rows_at // 8
    for g in range(2):
        col_ids = 16 * (member % 8) + 2 * (rows_at % 8) + g
        valid = jnp.logical_and(row_ids < height, col_ids < width)
        bias[g] = jnp.where(valid, 0.0, -jnp.inf).astype(F32)

    arrive(0)
    exchange(1)

    @pl.loop(0, 4)
    def _(i):
        tokens = split(came[0, pl.ds(pl.multiple_of(i * 128, 128), 128), :])
        for g in range(2):
            part = pl.ds(pl.multiple_of(g * MEMBERS + i * 64, 64), 64)
            centered = tokens[g] - jnp.mean(tokens[g], axis=-1, keepdims=True)
            scale = lax.rsqrt(jnp.mean(centered * centered, axis=-1, keepdims=True) + EPSILON)
            unit_rows = centered * scale
            unit[part, :] = unit_rows
            inv[part, :] = jnp.broadcast_to(scale, (64, 128))
            att[part, :] = unit_rows.astype(BF16)

    @pl.loop(0, 6)
    def _(i):
        part = pl.ds(pl.multiple_of(i * 128, 128), 128)
        normed_t[part, :] = att[:, part].T

    lane = lax.broadcasted_iota(jnp.int32, (MEMBERS, 128), 1) // HEAD_DIM
    to_exp2 = ROOT * math.log2(math.e)

    def one_head(value, j):
        return jnp.where(lane == j, value, jnp.zeros_like(value))

    def feature(i, size=128):
        return pl.ds(pl.multiple_of(i, size), size)

    def project(block):
        for n in range(3):
            tile = dot(att[...], weights[block, :, :, pl.ds(256 * n, 256)].reshape(D, 256)).astype(BF16)
            qkv[:, pl.ds(block * D + 256 * n, 256)] = tile
            if n > 0:
                kv_t[block, pl.ds(256 * (n - 1), 256), :] = tile.T

    def attend(block):
        @pl.loop(0, 4)
        def _(i):
            g, quad = i // 2, i % 2
            mine = feature(g * MEMBERS, MEMBERS)
            queries = qkv[mine, feature(block * D + quad * 128)]
            keys = qkv[mine, feature(block * D + 256 + quad * 128)]
            shift = bias[g]
            shift = jnp.concatenate([shift, shift], axis=1)
            for j in range(4):
                scores = dot_last(one_head(keys, j), queries) * to_exp2 + shift
                shifted = jnp.exp2(scores - jnp.max(scores, axis=0, keepdims=True))
                low = (shifted * (1.0 / jnp.sum(shifted, axis=0, keepdims=True))).astype(BF16)
                chances[(block * 4 + i) * 4 + j] = low
                values_t = kv_t[block, feature(256 + quad * 128 + j * 32, 32), mine]
                att_t[feature(block * 256 + quad * 128 + j * 32, 32), mine] = dot(values_t, low).astype(BF16)

    weights_there(0)
    project(0)
    project(1)
    attend(0)
    weights_core_far(1)
    attend(1)
    weights_there(1)
    project(2)
    attend(2)

    @pl.loop(0, 6)
    def _(i):
        part = feature(i * 128)
        att[:, part] = att_t[part, :].T

    for i in range(3):
        part = pl.ds(256 * i, 256)
        wide[:, part] = dot(att[...], weights[3, :, :, part].reshape(D, 256))

    @pl.loop(0, 4)
    def _(i):
        both = feature(i * 128)
        first = wide[feature(i * 64, 64), :]
        second = wide[feature(MEMBERS + i * 64, 64), :]
        sent[2, both, :] = (came[0, both, :].astype(F32) + merge(first, second)).astype(BF16)

    exchange(2)

    active = zl == x_at // 2
    owner = jnp.logical_and(active, zh < 3)
    mine48 = pl.ds(pl.multiple_of((x_at % 2) * 48, 16), 48)

    def start_core(b):
        push(
            terms.at[b, :, pl.ds(pl.multiple_of((1 - core) * HALF, 128), HALF)],
            core_in.at[b],
            r_send.at[b, 0],
            r_recv.at[b, 0],
            device(c=1 - core),
        )

    def add_core(b):
        wait(core_in.at[b], r_recv.at[b, 0])
        for l in range(2):
            for y in range(4):
                src, dst = pl.ds((l * 4 + y) * 96, 96), pl.ds((y * 2 + l) * 96, 96)
                cols = pl.ds(pl.multiple_of(core * HALF, 128), HALF)
                core_sum[b, dst, :] = (
                    terms[b, src, cols].astype(F32) + core_in[b, src, :].astype(F32)
                ).astype(BF16)

    def start_y(b):
        add_core(b)
        for k in range(1, 4):
            y = (y_at + k) % 4
            src = core_sum.at[b, pl.ds(pl.multiple_of(y * 192, 16), 192)]
            push(src, y_in.at[b, k - 1], r_send.at[b, 1], r_recv.at[b, 1], device(y=y))

    def start_x(b):
        wait(y_in.at[b], r_recv.at[b, 1])
        acc = core_sum[b, pl.ds(pl.multiple_of(y_at * 192, 16), 192), :].astype(F32)
        for k in range(3):
            acc = acc + y_in[b, k].astype(F32)
        y_sum[b] = acc.astype(BF16)
        for k in range(1, 4):
            x = (x_at + k) % 4
            src = y_sum.at[b, pl.ds(pl.multiple_of(x * 48, 16), 48)]
            push(src, x_in.at[b, k - 1], r_send.at[b, 5], r_recv.at[b, 5], device(x=x))

    def start_z(b):
        wait(x_in.at[b], r_recv.at[b, 5])
        acc = y_sum[b, pl.ds(pl.multiple_of(x_at * 48, 16), 48), :].astype(F32)
        for k in range(3):
            acc = acc + x_in[b, k].astype(F32)
        x_sum[b] = acc.astype(BF16)
        for j in range(3):
            rows = pl.ds(16 * j, 16)

            @pl.when(jnp.logical_not(jnp.logical_and(active, zh == j)))
            def _():
                to = device(h=j, l=x_at // 2)
                push(x_sum.at[b, rows], z_in.at[b, zh * 2 + zl], r_send.at[b, 2], r_recv.at[b, 2], to)

            @pl.when(jnp.logical_and(active, zh == j))
            def _():
                z_in[b, zh * 2 + zl] = x_sum[b, rows, :]

    def start_regather(b):
        @pl.when(owner)
        def _():
            wait(z_in.at[b, pl.ds(0, 7)], r_recv.at[b, 2])
            acc = z_in[b, 0].astype(F32)
            for k in range(1, 8):
                acc = acc + z_in[b, k].astype(F32)
            rows = pl.ds(pl.multiple_of(zh * 16, 16), 16)
            total[b, rows, :] = acc.astype(BF16)
            for k in range(1, 4):
                to = device(h=(zh + k) % 4)
                push(total.at[b, rows], total.at[b, rows], r_send.at[b, 3], r_recv.at[b, 3], to)

    def start_xy(b):
        add_core(b)

        @pl.loop(1, 16)
        def _(k):
            x, y = (x_at + k % 4) % 4, (y_at + k // 4) % 4
            src = core_sum.at[b, pl.ds(pl.multiple_of(y * 192 + x * 48, 16), 48)]
            push(src, xy_in.at[k - 1], r_send.at[b, 1], r_recv.at[b, 1], device(x=x, y=y))

    def start_all(b):
        wait(xy_in, r_recv.at[b, 1])
        acc = core_sum[b, pl.ds(pl.multiple_of(y_at * 192 + x_at * 48, 16), 48), :].astype(F32)
        for k in range(15):
            acc = acc + xy_in[k].astype(F32)
        low = acc.astype(BF16)
        x_sum[b] = low
        slot = all_in.at[zh * 2 + zl]
        for k in range(1, 4):
            to = device(h=(zh + k) % 4, l=x_at // 2)
            push(x_sum.at[b], slot, r_send.at[b, 2], r_recv.at[b, 2], to)

        @pl.when(jnp.logical_not(active))
        def _():
            push(x_sum.at[b], slot, r_send.at[b, 3], r_recv.at[b, 2], device(l=1 - zl))

        @pl.when(active)
        def _():
            all_in[zh * 2 + zl] = low

    def spread(b):
        for k in range(1, 8):
            to = device(x=(x_at + k // 2) % 4, c=(core + k) % 2)
            push(total.at[b], whole.at[b, core, mine48], r_send.at[b, 4], r_recv.at[b, 4], to)
        whole[b, core, mine48, :] = total[b]

    def start_spread_all(b):
        @pl.when(active)
        def _():
            wait(all_in.at[pl.ds(0, 7)], r_recv.at[b, 2])
            acc = all_in[0].astype(F32)
            for k in range(1, 8):
                acc = acc + all_in[k].astype(F32)
            total[b] = acc.astype(BF16)
            spread(b)

    def start_spread(b):
        @pl.when(active)
        def _():
            @pl.when(zh < 3)
            def _():
                wait(total.at[b, pl.ds(0, 32)], r_recv.at[b, 3])

            @pl.when(zh == 3)
            def _():
                wait(total.at[b], r_recv.at[b, 3])

            spread(b)

    def finish_terms(b):
        @pl.when(active)
        def _():
            wait(core_in.at[b, pl.ds(0, 144)], r_recv.at[b, 4])

        @pl.when(jnp.logical_not(active))
        def _():
            wait(core_in.at[b, pl.ds(0, 192)], r_recv.at[b, 4])

        full = jnp.concatenate([whole[b, 0], whole[b, 1]], axis=1)
        if b == 0:
            wg_ref[:, pl.ds(3 * D, D)] = full
        else:
            for n in range(3):
                wg_ref[:, pl.ds(n * D + (b - 1) * 256, 256)] = full[:, n * 256 : (n + 1) * 256]

    def settle_terms(b):
        wait(core_in.at[b], r_send.at[b, 0])
        if b == 3:
            wait(xy_in, r_send.at[b, 1])
            wait(all_in.at[pl.ds(0, 3)], r_send.at[b, 2])

            @pl.when(jnp.logical_not(active))
            def _():
                wait(x_sum.at[b], r_send.at[b, 3])

        else:
            wait(y_in.at[b], r_send.at[b, 1])
            wait(x_in.at[b], r_send.at[b, 5])

            @pl.when(owner)
            def _():
                wait(z_in.at[b, pl.ds(0, 2)], r_send.at[b, 2])
                wait(z_in.at[b, pl.ds(0, 3)], r_send.at[b, 3])

            @pl.when(jnp.logical_not(owner))
            def _():
                wait(z_in.at[b, pl.ds(0, 3)], r_send.at[b, 2])

        @pl.when(active)
        def _():
            wait(core_in.at[b, pl.ds(0, 336)], r_send.at[b, 4])

    arrive(1)

    @pl.loop(0, 4)
    def _(i):
        grads = split(came[1, feature(i * 128), :])
        for g in range(2):
            part = feature(g * MEMBERS + i * 64, 64)
            keep = bias[g, feature(i * 64, 64), :] == 0.0
            keep = jnp.concatenate([keep.astype(F32)] * 6, axis=1)
            masked[part, :] = (grads[g] * keep).astype(BF16)

    for i in range(3):
        part = pl.ds(256 * i, 256)
        out_grad[:, part] = dot_last(masked[...], block_weights(3)[256 * i : 256 * i + 256]).astype(BF16)
    for i in range(3):
        part = pl.ds(256 * i, 256)
        terms[0, :, part] = dot(att_t[...], masked[:, part]).astype(BF16)
    start_core(0)

    def attend_back(block, g):
        @pl.loop(0, 2)
        def _(quad):
            mine = feature(g * MEMBERS, MEMBERS)
            queries = qkv[mine, feature(block * D + quad * 128)]
            values = qkv[mine, feature(block * D + 512 + quad * 128)]
            grads = out_grad[mine, feature(block * 256 + quad * 128)]
            key_grad = jnp.zeros((MEMBERS, 128), F32)
            value_grad = jnp.zeros((MEMBERS, 128), F32)
            query_grad = []
            for j in range(4):
                chance_grad = dot_last(one_head(values, j), grads)
                low = chances[(block * 4 + g * 2 + quad) * 4 + j]
                chance = low.astype(F32)
                spread = jnp.sum(chance * chance_grad, axis=0, keepdims=True)
                score_grad = (chance * (chance_grad - spread) * ROOT).astype(BF16)
                value_grad += dot(low, one_head(grads, j))
                key_grad += dot(score_grad, one_head(queries, j))
                keys_t = kv_t[block, feature(quad * 128 + j * 32, 32), mine]
                query_grad.append(dot(keys_t, score_grad))
            query_grad = jnp.concatenate(query_grad, axis=0).astype(BF16)
            proj_grad[mine, feature(block * D + quad * 128)] = query_grad.T
            proj_grad[mine, feature(block * D + 256 + quad * 128)] = key_grad.astype(BF16)
            proj_grad[mine, feature(block * D + 512 + quad * 128)] = value_grad.astype(BF16)

    def weight_terms(block):
        for n in range(3):
            cols = pl.ds(block * D + n * 256, 256)
            terms[block + 1, :, pl.ds(n * 256, 256)] = dot(normed_t[...], proj_grad[:, cols]).astype(BF16)

    attend_back(0, 0)
    start_y(0)
    attend_back(0, 1)
    weight_terms(0)
    start_core(1)
    attend_back(1, 0)
    start_y(1)
    attend_back(1, 1)
    weight_terms(1)
    start_core(2)
    start_x(0)
    attend_back(2, 0)
    start_y(2)
    start_z(0)
    attend_back(2, 1)
    weight_terms(2)
    start_core(3)
    start_x(1)
    for i in range(3):
        part = pl.ds(256 * i, 256)
        grad = jnp.zeros((TOKENS, 256), F32)
        for b in range(3):
            grad += dot_last(proj_grad[:, pl.ds(b * D, D)], block_weights(b)[256 * i : 256 * i + 256])
        wide[:, part] = grad
    start_xy(3)
    start_regather(0)

    @pl.loop(0, 4)
    def _(i):
        both = feature(i * 128)
        parts = []
        for g in range(2):
            part = feature(g * MEMBERS + i * 64, 64)
            grad, unit_rows = wide[part, :], unit[part, :]
            moved = (
                grad
                - jnp.mean(grad, axis=-1, keepdims=True)
                - unit_rows * jnp.mean(grad * unit_rows, axis=-1, keepdims=True)
            )
            scale = jnp.concatenate([inv[part, :]] * 6, axis=1)
            parts.append(masked[part, :].astype(F32) + scale * moved)
        sent[3, both, :] = merge(*parts).astype(BF16)

    start_x(2)
    start_z(1)
    exchange(3, 0, 1, 12)
    arrive(2)
    reorder(scatter, came.at[2], out_ref)
    start_z(2)
    start_spread(0)
    start_regather(1)
    start_all(3)
    start_regather(2)
    exchange(3, 1, 12, 32)
    start_spread(1)
    finish_terms(0)
    start_spread(2)
    start_spread_all(3)
    finish_terms(1)
    finish_terms(2)
    finish_terms(3)
    arrive(3)
    reorder(scatter, came.at[3], ig_ref)
    left(3, 0, 11)
    left(3, 1, 20)

    for t in range(4):
        if t < 3:
            left(t, 0, 31)
        settle_terms(t)
    for p in range(2):
        weights_settle(p)


def per_device(inputs, cotangent, extents, weights):
    shape = inputs.shape
    vmem = pl.BlockSpec(memory_space=pltpu.VMEM)
    out, ig, wg = pl.pallas_call(
        kernel,
        out_shape=(
            jax.ShapeDtypeStruct((TOKENS, D), BF16),
            jax.ShapeDtypeStruct((TOKENS, D), BF16),
            jax.ShapeDtypeStruct((96, 4 * D), BF16),
        ),
        in_specs=[pl.BlockSpec(memory_space=pltpu.SMEM), vmem, vmem, vmem],
        out_specs=(vmem, vmem, vmem),
        scratch_shapes=[
            pltpu.VMEM((4, TOKENS, D), BF16),
            pltpu.VMEM((4, TOKENS, D), BF16),
            pltpu.VMEM((4, 8, 96, D), BF16),
            pltpu.VMEM((TOKENS, D), F32),
            pltpu.VMEM((TOKENS, 128), F32),
            pltpu.VMEM((D, TOKENS), BF16),
            pltpu.VMEM((TOKENS, 3 * D), BF16),
            pltpu.VMEM((3, TOKENS, TOKENS), BF16),
            pltpu.VMEM((2, MEMBERS, 128), F32),
            pltpu.VMEM((2 * HEADS, MEMBERS, MEMBERS), BF16),
            pltpu.VMEM((D, TOKENS), BF16),
            pltpu.VMEM((TOKENS, D), BF16),
            pltpu.VMEM((TOKENS, D), BF16),
            pltpu.VMEM((TOKENS, D), BF16),
            pltpu.VMEM((TOKENS, 3 * D), BF16),
            pltpu.VMEM((TOKENS, D), F32),
            pltpu.VMEM((4, D, D), BF16),
            pltpu.VMEM((4, D, HALF), BF16),
            pltpu.VMEM((4, D, HALF), BF16),
            pltpu.VMEM((4, 3, 192, HALF), BF16),
            pltpu.VMEM((4, 192, HALF), BF16),
            pltpu.VMEM((4, 3, 48, HALF), BF16),
            pltpu.VMEM((4, 48, HALF), BF16),
            pltpu.VMEM((4, 8, 16, HALF), BF16),
            pltpu.VMEM((15, 48, HALF), BF16),
            pltpu.VMEM((8, 48, HALF), BF16),
            pltpu.VMEM((4, 48, HALF), BF16),
            pltpu.VMEM((4, 2, 96, HALF), BF16),
            pltpu.SemaphoreType.DMA((4, 2)),
            pltpu.SemaphoreType.DMA((4,)),
            pltpu.SemaphoreType.DMA((2, 5)),
            pltpu.SemaphoreType.DMA((2, 5)),
            pltpu.SemaphoreType.DMA((4, 6)),
            pltpu.SemaphoreType.DMA((4, 6)),
        ],
        compiler_params=pltpu.CompilerParams(
            collective_id=0, has_side_effects=True, vmem_limit_bytes=60 << 20
        ),
    )(extents, inputs.reshape(TOKENS, D), cotangent.reshape(TOKENS, D), weights)
    return out.reshape(shape), ig.reshape(shape), wg.astype(F32)


def solution(mesh):
    placed = (
        P("dp", "rows", None, None),
        P("dp", "rows", None, None),
        P("dp", None),
        P("dp", None),
    )
    return jax.shard_map(
        per_device,
        mesh=mesh,
        in_specs=placed,
        out_specs=(P("dp", "rows", None, None), P("dp", "rows", None, None), P("dp", None)),
        check_vma=False,
    )
```

```python
import math

import jax
import jax.numpy as jnp
from jax import lax
from jax.experimental import pallas as pl
from jax.experimental.pallas import tpu as pltpu
from jax.sharding import PartitionSpec as P

MESH = pl.DeviceIdType.MESH
BF16 = jnp.bfloat16
F32 = jnp.float32

D = 768
HEADS = 24
HEAD_DIM = 32
TOKENS = 512
MEMBERS = 256
HALF = 384
ROOT = HEAD_DIM ** (-0.5)
EPSILON = 1e-05

CONTRACT_LAST = (((1,), (1,)), ((), ()))


def dot(a, b):
    return jnp.dot(a, b, preferred_element_type=F32)


def dot_last(a, b):
    return lax.dot_general(a, b, CONTRACT_LAST, preferred_element_type=F32)


def split(block):
    wide = block.astype(F32).reshape(8, 16, block.shape[-1])
    return [wide[:, 8 * g : 8 * g + 8, :].reshape(64, block.shape[-1]) for g in range(2)]


def merge(first, second):
    parts = [p.reshape(8, 8, p.shape[-1]) for p in (first, second)]
    return jnp.concatenate(parts, axis=1).reshape(128, first.shape[-1])


def kernel(
    extent_ref,
    x_ref,
    g_ref,
    w_ref,
    out_ref,
    ig_ref,
    wg_ref,
    sent,
    came,
    weights,
    unit,
    inv,
    normed_t,
    qkv,
    kv_t,
    bias,
    chances,
    att_t,
    att,
    masked,
    out_grad,
    proj_grad,
    wide,
    terms,
    core_in,
    core_sum,
    y_in,
    y_sum,
    x_in,
    x_sum,
    z_in,
    xy_in,
    all_in,
    total,
    whole,
    a_send,
    a_recv,
    w_send,
    w_recv,
    r_send,
    r_recv,
):
    rows_at = lax.axis_index("rows")
    dp_at = lax.axis_index("dp")
    x_at, zh, core = rows_at // 8, (rows_at // 2) % 4, rows_at % 2
    zl, y_at = dp_at // 4, dp_at % 4

    def device(x=None, h=None, c=None, l=None, y=None):
        x = x_at if x is None else x
        h = zh if h is None else h
        c = core if c is None else c
        l = zl if l is None else l
        y = y_at if y is None else y
        return (x * 8 + h * 2 + c, l * 4 + y)

    def push(src, dst, send, recv, to):
        pltpu.make_async_remote_copy(
            src_ref=src, dst_ref=dst, send_sem=send, recv_sem=recv, device_id=to, device_id_type=MESH
        ).start()

    def wait(ref, sem):
        pltpu.make_async_copy(ref, ref, sem).wait()

    def at16(i, size=16):
        return pl.ds(pl.multiple_of(i * 16, 16), size)

    for b in range(3):
        for n in range(3):
            weights[b, dp_at, :, pl.ds(n * 256, 256)] = w_ref[:, pl.ds(n * D + b * 256, 256)]
    weights[3, dp_at] = w_ref[:, pl.ds(3 * D, D)]
    barrier = pltpu.get_barrier_semaphore()

    @pl.loop(1, 32)
    def _(k):
        pl.semaphore_signal(
            barrier, inc=1, device_id=((rows_at + k) % 32, dp_at), device_id_type=MESH
        )

    @pl.loop(1, 8)
    def _(k):
        pl.semaphore_signal(
            barrier, inc=1, device_id=(rows_at, (dp_at + k) % 8), device_id_type=MESH
        )

    side = (zh + 3 + 2 * zl) % 4

    @pl.loop(1, 4)
    def _(k):
        for to in (
            device(x=(x_at + 1) % 4, y=(y_at + k) % 4),
            device(x=(x_at + 2) % 4, y=(y_at + k) % 4),
            device(x=(x_at + 3) % 4, y=(y_at + k) % 4),
            device(h=(zh + k) % 4, l=1 - zl),
            device(h=side, l=1 - zl, y=(y_at + k) % 4),
        ):
            pl.semaphore_signal(barrier, inc=1, device_id=to, device_id_type=MESH)

    to_row = lax.broadcasted_iota(jnp.int32, (128, 128), 0)
    from_row = lax.broadcasted_iota(jnp.int32, (128, 128), 1)
    gather = (from_row == (to_row % 8) * 16 + to_row // 8).astype(BF16)
    scatter = (from_row == (to_row % 16) * 8 + to_row // 16).astype(BF16)

    def reorder(matrix, src, dst):
        for i in range(4):
            part = pl.ds(128 * i, 128)
            dst[part, :] = dot(matrix, src[part, :]).astype(BF16)

    def exchange(t, part=0, first=1, last=32):
        @pl.loop(first, last)
        def _(k):
            kc, kx, kz = k // 16, (k // 4) % 4, k % 4
            peer = ((x_at + kx) % 4) * 8 + ((zh + kz) % 4) * 2 + (core + kc) % 2
            push(
                sent.at[t, at16(peer)],
                came.at[t, at16(rows_at)],
                a_send.at[t, part],
                a_recv.at[t],
                (peer, dp_at),
            )

        if part == 0:
            came[t, at16(rows_at), :] = sent[t, at16(rows_at), :]

    def left(t, part, count):
        wait(came.at[t, pl.ds(0, 16 * count)], a_send.at[t, part])

    def arrive(t):
        wait(came.at[t, pl.ds(0, 496)], a_recv.at[t])

    reorder(gather, x_ref, sent.at[0])
    pl.semaphore_wait(barrier, 53)

    piece = (pl.ds(pl.multiple_of((x_at // 2) * 48, 16), 48), pl.ds(pl.multiple_of((x_at % 2) * HALF, 128), HALF))
    near, far = pl.ds(zl * 4, 4), pl.ds((1 - zl) * 4, 4)

    def weights_far(p):
        mine = weights.at[2 * p + core, dp_at, piece[0], piece[1]]
        for k in range(4):
            to = device(h=zh if k < 2 else side, l=1 - zl, y=(y_at + k) % 4)
            push(mine, mine, w_send.at[p, 0], w_recv.at[p, 0], to)

    def weights_near(p):
        mine = weights.at[2 * p + core, dp_at]
        for k in range(1, 4):
            push(mine, mine, w_send.at[p, 1], w_recv.at[p, 1], device(y=(y_at + k) % 4))

    def weights_across(p):
        mine = weights.at[2 * p + core, far, piece[0], piece[1]]
        wait(mine, w_recv.at[p, 0])
        for k in range(1, 4):
            push(mine, mine, w_send.at[p, 2], w_recv.at[p, 2], device(x=(x_at + k) % 4))

    def weights_core_near(p):
        mine = weights.at[2 * p + core, near]
        wait(weights.at[2 * p, pl.ds(0, 3)], w_recv.at[p, 1])
        push(mine, mine, w_send.at[p, 3], w_recv.at[p, 3], device(c=1 - core))

    def weights_core_far(p):
        mine = weights.at[2 * p + core, far]
        wait(weights.at[2 * p, pl.ds(0, 3)], w_recv.at[p, 2])
        push(mine, mine, w_send.at[p, 4], w_recv.at[p, 4], device(c=1 - core))

    def weights_there(p):
        wait(weights.at[2 * p, near], w_recv.at[p, 3])
        wait(weights.at[2 * p, far], w_recv.at[p, 4])

    def weights_settle(p):
        wait(weights.at[2 * p, far, piece[0], piece[1]], w_send.at[p, 0])
        wait(weights.at[2 * p, pl.ds(0, 3)], w_send.at[p, 1])
        wait(weights.at[2 * p, pl.ds(0, 3)], w_send.at[p, 2])
        wait(weights.at[2 * p, near], w_send.at[p, 3])
        wait(weights.at[2 * p, far], w_send.at[p, 4])

    def block_weights(b):
        return weights[b].reshape(D, D)

    weights_far(0)
    weights_near(0)
    exchange(0)
    weights_across(0)
    weights_far(1)
    weights_near(1)
    reorder(gather, g_ref, sent.at[1])
    weights_core_near(0)
    weights_core_far(0)
    weights_across(1)
    weights_core_near(1)

    height, width = extent_ref[0, 0], extent_ref[0, 1]
    member = lax.broadcasted_iota(jnp.int32, (MEMBERS, 128), 0)
    row_ids = 4 * (member // 8) + rows_at // 8
    for g in range(2):
        col_ids = 16 * (member % 8) + 2 * (rows_at % 8) + g
        valid = jnp.logical_and(row_ids < height, col_ids < width)
        bias[g] = jnp.where(valid, 0.0, -jnp.inf).astype(F32)

    arrive(0)
    exchange(1)

    @pl.loop(0, 4)
    def _(i):
        tokens = split(came[0, pl.ds(pl.multiple_of(i * 128, 128), 128), :])
        for g in range(2):
            part = pl.ds(pl.multiple_of(g * MEMBERS + i * 64, 64), 64)
            centered = tokens[g] - jnp.mean(tokens[g], axis=-1, keepdims=True)
            scale = lax.rsqrt(jnp.mean(centered * centered, axis=-1, keepdims=True) + EPSILON)
            unit_rows = centered * scale
            unit[part, :] = unit_rows
            inv[part, :] = jnp.broadcast_to(scale, (64, 128))
            att[part, :] = unit_rows.astype(BF16)

    @pl.loop(0, 6)
    def _(i):
        part = pl.ds(pl.multiple_of(i * 128, 128), 128)
        normed_t[part, :] = att[:, part].T

    lane = lax.broadcasted_iota(jnp.int32, (MEMBERS, 128), 1) // HEAD_DIM
    to_exp2 = ROOT * math.log2(math.e)

    def one_head(value, j):
        return jnp.where(lane == j, value, jnp.zeros_like(value))

    def feature(i, size=128):
        return pl.ds(pl.multiple_of(i, size), size)

    def project(block):
        for n in range(3):
            tile = dot(att[...], weights[block, :, :, pl.ds(256 * n, 256)].reshape(D, 256)).astype(BF16)
            qkv[:, pl.ds(block * D + 256 * n, 256)] = tile
            if n > 0:
                kv_t[block, pl.ds(256 * (n - 1), 256), :] = tile.T

    def attend(block):
        @pl.loop(0, 4)
        def _(i):
            g, quad = i // 2, i % 2
            mine = feature(g * MEMBERS, MEMBERS)
            queries = qkv[mine, feature(block * D + quad * 128)]
            keys = qkv[mine, feature(block * D + 256 + quad * 128)]
            shift = bias[g]
            shift = jnp.concatenate([shift, shift], axis=1)
            for j in range(4):
                scores = dot_last(one_head(keys, j), queries) * to_exp2 + shift
                shifted = jnp.exp2(scores - jnp.max(scores, axis=0, keepdims=True))
                low = (shifted * (1.0 / jnp.sum(shifted, axis=0, keepdims=True))).astype(BF16)
                chances[(block * 4 + i) * 4 + j] = low
                values_t = kv_t[block, feature(256 + quad * 128 + j * 32, 32), mine]
                att_t[feature(block * 256 + quad * 128 + j * 32, 32), mine] = dot(values_t, low).astype(BF16)

    weights_there(0)
    project(0)
    project(1)
    attend(0)
    weights_core_far(1)
    attend(1)
    weights_there(1)
    project(2)
    attend(2)

    @pl.loop(0, 6)
    def _(i):
        part = feature(i * 128)
        att[:, part] = att_t[part, :].T

    for i in range(3):
        part = pl.ds(256 * i, 256)
        wide[:, part] = dot(att[...], weights[3, :, :, part].reshape(D, 256))

    @pl.loop(0, 4)
    def _(i):
        both = feature(i * 128)
        first = wide[feature(i * 64, 64), :]
        second = wide[feature(MEMBERS + i * 64, 64), :]
        sent[2, both, :] = (came[0, both, :].astype(F32) + merge(first, second)).astype(BF16)

    exchange(2)

    active = zl == x_at // 2
    owner = jnp.logical_and(active, zh < 3)
    mine48 = pl.ds(pl.multiple_of((x_at % 2) * 48, 16), 48)

    def start_core(b):
        push(
            terms.at[b, :, pl.ds(pl.multiple_of((1 - core) * HALF, 128), HALF)],
            core_in.at[b],
            r_send.at[b, 0],
            r_recv.at[b, 0],
            device(c=1 - core),
        )

    def add_core(b):
        wait(core_in.at[b], r_recv.at[b, 0])
        for l in range(2):
            for y in range(4):
                src, dst = pl.ds((l * 4 + y) * 96, 96), pl.ds((y * 2 + l) * 96, 96)
                cols = pl.ds(pl.multiple_of(core * HALF, 128), HALF)
                core_sum[b, dst, :] = (
                    terms[b, src, cols].astype(F32) + core_in[b, src, :].astype(F32)
                ).astype(BF16)

    def start_y(b):
        add_core(b)
        for k in range(1, 4):
            y = (y_at + k) % 4
            src = core_sum.at[b, pl.ds(pl.multiple_of(y * 192, 16), 192)]
            push(src, y_in.at[b, k - 1], r_send.at[b, 1], r_recv.at[b, 1], device(y=y))

    def start_x(b):
        wait(y_in.at[b], r_recv.at[b, 1])
        acc = core_sum[b, pl.ds(pl.multiple_of(y_at * 192, 16), 192), :].astype(F32)
        for k in range(3):
            acc = acc + y_in[b, k].astype(F32)
        y_sum[b] = acc.astype(BF16)
        for k in range(1, 4):
            x = (x_at + k) % 4
            src = y_sum.at[b, pl.ds(pl.multiple_of(x * 48, 16), 48)]
            push(src, x_in.at[b, k - 1], r_send.at[b, 5], r_recv.at[b, 5], device(x=x))

    def start_z(b):
        wait(x_in.at[b], r_recv.at[b, 5])
        acc = y_sum[b, pl.ds(pl.multiple_of(x_at * 48, 16), 48), :].astype(F32)
        for k in range(3):
            acc = acc + x_in[b, k].astype(F32)
        x_sum[b] = acc.astype(BF16)
        for j in range(3):
            rows = pl.ds(16 * j, 16)

            @pl.when(jnp.logical_not(jnp.logical_and(active, zh == j)))
            def _():
                to = device(h=j, l=x_at // 2)
                push(x_sum.at[b, rows], z_in.at[b, zh * 2 + zl], r_send.at[b, 2], r_recv.at[b, 2], to)

            @pl.when(jnp.logical_and(active, zh == j))
            def _():
                z_in[b, zh * 2 + zl] = x_sum[b, rows, :]

    def start_regather(b):
        @pl.when(owner)
        def _():
            wait(z_in.at[b, pl.ds(0, 7)], r_recv.at[b, 2])
            acc = z_in[b, 0].astype(F32)
            for k in range(1, 8):
                acc = acc + z_in[b, k].astype(F32)
            rows = pl.ds(pl.multiple_of(zh * 16, 16), 16)
            total[b, rows, :] = acc.astype(BF16)
            for k in range(1, 4):
                to = device(h=(zh + k) % 4)
                push(total.at[b, rows], total.at[b, rows], r_send.at[b, 3], r_recv.at[b, 3], to)

    def start_xy(b):
        add_core(b)

        @pl.loop(1, 16)
        def _(k):
            x, y = (x_at + k % 4) % 4, (y_at + k // 4) % 4
            src = core_sum.at[b, pl.ds(pl.multiple_of(y * 192 + x * 48, 16), 48)]
            push(src, xy_in.at[k - 1], r_send.at[b, 1], r_recv.at[b, 1], device(x=x, y=y))

    def start_all(b):
        wait(xy_in, r_recv.at[b, 1])
        acc = core_sum[b, pl.ds(pl.multiple_of(y_at * 192 + x_at * 48, 16), 48), :].astype(F32)
        for k in range(15):
            acc = acc + xy_in[k].astype(F32)
        low = acc.astype(BF16)
        x_sum[b] = low
        slot = all_in.at[zh * 2 + zl]
        for k in range(1, 4):
            to = device(h=(zh + k) % 4, l=x_at // 2)
            push(x_sum.at[b], slot, r_send.at[b, 2], r_recv.at[b, 2], to)

        @pl.when(jnp.logical_not(active))
        def _():
            push(x_sum.at[b], slot, r_send.at[b, 3], r_recv.at[b, 2], device(l=1 - zl))

        @pl.when(active)
        def _():
            all_in[zh * 2 + zl] = low

    def spread(b):
        for k in range(1, 8):
            to = device(x=(x_at + k // 2) % 4, c=(core + k) % 2)
            push(total.at[b], whole.at[b, core, mine48], r_send.at[b, 4], r_recv.at[b, 4], to)
        whole[b, core, mine48, :] = total[b]

    def start_spread_all(b):
        @pl.when(active)
        def _():
            wait(all_in.at[pl.ds(0, 7)], r_recv.at[b, 2])
            acc = all_in[0].astype(F32)
            for k in range(1, 8):
                acc = acc + all_in[k].astype(F32)
            total[b] = acc.astype(BF16)
            spread(b)

    def start_spread(b):
        @pl.when(active)
        def _():
            @pl.when(zh < 3)
            def _():
                wait(total.at[b, pl.ds(0, 32)], r_recv.at[b, 3])

            @pl.when(zh == 3)
            def _():
                wait(total.at[b], r_recv.at[b, 3])

            spread(b)

    def finish_terms(b):
        @pl.when(active)
        def _():
            wait(core_in.at[b, pl.ds(0, 144)], r_recv.at[b, 4])

        @pl.when(jnp.logical_not(active))
        def _():
            wait(core_in.at[b, pl.ds(0, 192)], r_recv.at[b, 4])

        full = jnp.concatenate([whole[b, 0], whole[b, 1]], axis=1)
        if b == 0:
            wg_ref[:, pl.ds(3 * D, D)] = full
        else:
            for n in range(3):
                wg_ref[:, pl.ds(n * D + (b - 1) * 256, 256)] = full[:, n * 256 : (n + 1) * 256]

    def settle_terms(b):
        wait(core_in.at[b], r_send.at[b, 0])
        if b == 3:
            wait(xy_in, r_send.at[b, 1])
            wait(all_in.at[pl.ds(0, 3)], r_send.at[b, 2])

            @pl.when(jnp.logical_not(active))
            def _():
                wait(x_sum.at[b], r_send.at[b, 3])

        else:
            wait(y_in.at[b], r_send.at[b, 1])
            wait(x_in.at[b], r_send.at[b, 5])

            @pl.when(owner)
            def _():
                wait(z_in.at[b, pl.ds(0, 2)], r_send.at[b, 2])
                wait(z_in.at[b, pl.ds(0, 3)], r_send.at[b, 3])

            @pl.when(jnp.logical_not(owner))
            def _():
                wait(z_in.at[b, pl.ds(0, 3)], r_send.at[b, 2])

        @pl.when(active)
        def _():
            wait(core_in.at[b, pl.ds(0, 336)], r_send.at[b, 4])

    arrive(1)

    @pl.loop(0, 4)
    def _(i):
        grads = split(came[1, feature(i * 128), :])
        for g in range(2):
            part = feature(g * MEMBERS + i * 64, 64)
            keep = bias[g, feature(i * 64, 64), :] == 0.0
            keep = jnp.concatenate([keep.astype(F32)] * 6, axis=1)
            masked[part, :] = (grads[g] * keep).astype(BF16)

    for i in range(3):
        part = pl.ds(256 * i, 256)
        out_grad[:, part] = dot_last(masked[...], block_weights(3)[256 * i : 256 * i + 256]).astype(BF16)
    for i in range(3):
        part = pl.ds(256 * i, 256)
        terms[0, :, part] = dot(att_t[...], masked[:, part]).astype(BF16)
    start_core(0)

    def attend_back(block, g):
        @pl.loop(0, 2)
        def _(quad):
            mine = feature(g * MEMBERS, MEMBERS)
            queries = qkv[mine, feature(block * D + quad * 128)]
            values = qkv[mine, feature(block * D + 512 + quad * 128)]
            grads = out_grad[mine, feature(block * 256 + quad * 128)]
            key_grad = jnp.zeros((MEMBERS, 128), F32)
            value_grad = jnp.zeros((MEMBERS, 128), F32)
            query_grad = []
            for j in range(4):
                chance_grad = dot_last(one_head(values, j), grads)
                low = chances[(block * 4 + g * 2 + quad) * 4 + j]
                chance = low.astype(F32)
                spread = jnp.sum(chance * chance_grad, axis=0, keepdims=True)
                score_grad = (chance * (chance_grad - spread) * ROOT).astype(BF16)
                value_grad += dot(low, one_head(grads, j))
                key_grad += dot(score_grad, one_head(queries, j))
                keys_t = kv_t[block, feature(quad * 128 + j * 32, 32), mine]
                query_grad.append(dot(keys_t, score_grad))
            query_grad = jnp.concatenate(query_grad, axis=0).astype(BF16)
            proj_grad[mine, feature(block * D + quad * 128)] = query_grad.T
            proj_grad[mine, feature(block * D + 256 + quad * 128)] = key_grad.astype(BF16)
            proj_grad[mine, feature(block * D + 512 + quad * 128)] = value_grad.astype(BF16)

    def weight_terms(block):
        for n in range(3):
            cols = pl.ds(block * D + n * 256, 256)
            terms[block + 1, :, pl.ds(n * 256, 256)] = dot(normed_t[...], proj_grad[:, cols]).astype(BF16)

    attend_back(0, 0)
    start_y(0)
    attend_back(0, 1)
    weight_terms(0)
    start_core(1)
    attend_back(1, 0)
    start_y(1)
    attend_back(1, 1)
    weight_terms(1)
    start_core(2)
    start_x(0)
    attend_back(2, 0)
    start_y(2)
    start_z(0)
    attend_back(2, 1)
    weight_terms(2)
    start_core(3)
    start_x(1)
    for i in range(3):
        part = pl.ds(256 * i, 256)
        grad = jnp.zeros((TOKENS, 256), F32)
        for b in range(3):
            grad += dot_last(proj_grad[:, pl.ds(b * D, D)], block_weights(b)[256 * i : 256 * i + 256])
        wide[:, part] = grad
    start_xy(3)
    start_regather(0)

    @pl.loop(0, 4)
    def _(i):
        both = feature(i * 128)
        parts = []
        for g in range(2):
            part = feature(g * MEMBERS + i * 64, 64)
            grad, unit_rows = wide[part, :], unit[part, :]
            moved = (
                grad
                - jnp.mean(grad, axis=-1, keepdims=True)
                - unit_rows * jnp.mean(grad * unit_rows, axis=-1, keepdims=True)
            )
            scale = jnp.concatenate([inv[part, :]] * 6, axis=1)
            parts.append(masked[part, :].astype(F32) + scale * moved)
        sent[3, both, :] = merge(*parts).astype(BF16)

    start_x(2)
    start_z(1)
    exchange(3, 0, 1, 12)
    arrive(2)
    reorder(scatter, came.at[2], out_ref)
    start_z(2)
    start_spread(0)
    start_regather(1)
    start_all(3)
    start_regather(2)
    exchange(3, 1, 12, 32)
    start_spread(1)
    finish_terms(0)
    start_spread(2)
    start_spread_all(3)
    finish_terms(1)
    finish_terms(2)
    finish_terms(3)
    arrive(3)
    reorder(scatter, came.at[3], ig_ref)
    left(3, 0, 11)
    left(3, 1, 20)

    for t in range(4):
        if t < 3:
            left(t, 0, 31)
        settle_terms(t)
    for p in range(2):
        weights_settle(p)


def per_device(inputs, cotangent, extents, weights):
    shape = inputs.shape
    vmem = pl.BlockSpec(memory_space=pltpu.VMEM)
    out, ig, wg = pl.pallas_call(
        kernel,
        out_shape=(
            jax.ShapeDtypeStruct((TOKENS, D), BF16),
            jax.ShapeDtypeStruct((TOKENS, D), BF16),
            jax.ShapeDtypeStruct((96, 4 * D), BF16),
        ),
        in_specs=[pl.BlockSpec(memory_space=pltpu.SMEM), vmem, vmem, vmem],
        out_specs=(vmem, vmem, vmem),
        scratch_shapes=[
            pltpu.VMEM((4, TOKENS, D), BF16),
            pltpu.VMEM((4, TOKENS, D), BF16),
            pltpu.VMEM((4, 8, 96, D), BF16),
            pltpu.VMEM((TOKENS, D), F32),
            pltpu.VMEM((TOKENS, 128), F32),
            pltpu.VMEM((D, TOKENS), BF16),
            pltpu.VMEM((TOKENS, 3 * D), BF16),
            pltpu.VMEM((3, TOKENS, TOKENS), BF16),
            pltpu.VMEM((2, MEMBERS, 128), F32),
            pltpu.VMEM((2 * HEADS, MEMBERS, MEMBERS), BF16),
            pltpu.VMEM((D, TOKENS), BF16),
            pltpu.VMEM((TOKENS, D), BF16),
            pltpu.VMEM((TOKENS, D), BF16),
            pltpu.VMEM((TOKENS, D), BF16),
            pltpu.VMEM((TOKENS, 3 * D), BF16),
            pltpu.VMEM((TOKENS, D), F32),
            pltpu.VMEM((4, D, D), BF16),
            pltpu.VMEM((4, D, HALF), BF16),
            pltpu.VMEM((4, D, HALF), BF16),
            pltpu.VMEM((4, 3, 192, HALF), BF16),
            pltpu.VMEM((4, 192, HALF), BF16),
            pltpu.VMEM((4, 3, 48, HALF), BF16),
            pltpu.VMEM((4, 48, HALF), BF16),
            pltpu.VMEM((4, 8, 16, HALF), BF16),
            pltpu.VMEM((15, 48, HALF), BF16),
            pltpu.VMEM((8, 48, HALF), BF16),
            pltpu.VMEM((4, 48, HALF), BF16),
            pltpu.VMEM((4, 2, 96, HALF), BF16),
            pltpu.SemaphoreType.DMA((4, 2)),
            pltpu.SemaphoreType.DMA((4,)),
            pltpu.SemaphoreType.DMA((2, 5)),
            pltpu.SemaphoreType.DMA((2, 5)),
            pltpu.SemaphoreType.DMA((4, 6)),
            pltpu.SemaphoreType.DMA((4, 6)),
        ],
        compiler_params=pltpu.CompilerParams(
            collective_id=0, has_side_effects=True, vmem_limit_bytes=60 << 20
        ),
    )(extents, inputs.reshape(TOKENS, D), cotangent.reshape(TOKENS, D), weights)
    return out.reshape(shape), ig.reshape(shape), wg.astype(F32)


def solution(mesh):
    placed = (
        P("dp", "rows", None, None),
        P("dp", "rows", None, None),
        P("dp", None),
        P("dp", None),
    )
    return jax.shard_map(
        per_device,
        mesh=mesh,
        in_specs=placed,
        out_specs=(P("dp", "rows", None, None), P("dp", "rows", None, None), P("dp", None)),
        check_vma=False,
    )
```
